32 devices in a mesh: groups: 2 (over x), dp: 16 (over z, y, core).
Axes of the slice: x: 2, y: 2, z: 4, core: 2. Of those that a mesh axis runs over, the one named last changes fastest.
Arguments:
- gate_preact: bfloat16 [1024, 28672], P('groups', 'dp'), parts along dimension 0, may hold values from -6 to 6
- up_preact: bfloat16 [1024, 28672], P('groups', 'dp'), parts along dimension 0, may hold values from -6 to 6
- out_grad: bfloat16 [1024, 8192], P(('groups', 'dp')), parts along dimension 0, may hold values from -6 to 6
- layer_input: bfloat16 [1024, 8192], P('groups', 'dp'), parts along dimension 0, may hold values from -6 to 6
- w_down: bfloat16 [28672, 8192], P('dp'), may hold values from -0.03125 to 0.03125
- proj_in_down: bfloat16 [64, 28672], P(None, 'dp'), may hold values from -0.03125 to 0.03125
- proj_out_down: bfloat16 [64, 8192], replicated, may hold values from -0.0625 to 0.0625
- proj_in_up: bfloat16 [64, 8192], P(None, 'dp'), may hold values from -0.0625 to 0.0625
- proj_out_up: bfloat16 [64, 28672], P(None, 'dp'), may hold values from -0.03125 to 0.03125
- queries: bfloat16 [2048, 8192], P('dp'), may hold values from -0.005859375 to 0.005859375
Outputs:
- scores: float32 [8, 2048], P('groups', 'dp'), parts along dimension 0
The draws below stay inside these ranges and needn't reach their ends.
There are 2 independent parts, one for each index of `groups`. The reference program is written for one: setup_inputs(seed, part) draws one part's arguments, and reference() takes and returns one part's arrays. A program takes and returns all parts, laid end to end along the dimension named above; an argument that names none is the same for every part. Nothing has to cross between parts.
All inputs are finite; a program needn't handle non-finite values.
Results may differ from the reference program's by a relative error of at most 0.0048.
Values may be sent and summed in bfloat16 or wider, within the bound.
A program may use at most 128 MiB of HBM per device.

```python
import jax
import jax.numpy as jnp
from jax import lax

D = 8192
FF = 28672
SKETCH = 64
SEQ_LEN = 128
TOKENS = 512
QUERIES = 2048


def level_of(stream_key, extent, shards, least, largest):
    def one(dim, shards_of):
        heights = jax.random.uniform(jax.random.fold_in(jax.random.fold_in(stream_key, 6), dim), (shards_of,), jnp.float32, least / len(shards), largest / len(shards))
        return jnp.repeat(jnp.exp(heights), extent[dim] // shards_of).reshape((-1,) + (1,) * (len(extent) - dim - 1))

    gain = one(*shards[0])
    for cut in shards[1:]:
        gain = gain * one(*cut)
    return gain


def normal_values(own_key, shape, width, reach, shards=(), kind=jnp.bfloat16):
    result = width * jax.random.normal(own_key, shape, jnp.float32)
    if shards:
        result = result * level_of(own_key, shape, shards, -0.22, 0.18)
    return jnp.clip(result, -reach, reach).astype(kind)


def setup_inputs(seed: int = 0, part: int = 0) -> dict:
    key_list = jax.random.split(jax.random.key(seed), 11)
    own_keys = jax.random.split(jax.random.fold_in(key_list[10], part), 11)
    gate_preact = normal_values(own_keys[0], (TOKENS, FF), 1.0, 6.0, ((1, 16),))
    up_preact = normal_values(own_keys[1], (TOKENS, FF), 1.0, 6.0, ((1, 16),))
    out_grad = normal_values(own_keys[2], (TOKENS, D), 1.0, 6.0, ((0, 16),))
    layer_input = normal_values(own_keys[3], (TOKENS, D), 1.0, 6.0, ((1, 16),))
    w_down = normal_values(key_list[4], (FF, D), FF ** -0.5, 0.03125, ((0, 16),))
    proj_in_down = normal_values(key_list[5], (SKETCH, FF), FF ** -0.5, 0.03125, ((1, 16),))
    proj_out_down = normal_values(key_list[6], (SKETCH, D), D ** -0.5, 0.0625)
    proj_in_up = normal_values(key_list[7], (SKETCH, D), D ** -0.5, 0.0625, ((1, 16),))
    proj_out_up = normal_values(key_list[8], (SKETCH, FF), FF ** -0.5, 0.03125, ((1, 16),))
    queries = normal_values(key_list[9], (QUERIES, 2 * SKETCH * SKETCH), (2 * SKETCH * SKETCH * SEQ_LEN) ** -0.5, 0.005859375, ((0, 16),))
    return {"gate_preact": gate_preact, "up_preact": up_preact, "out_grad": out_grad, "layer_input": layer_input, "w_down": w_down, "proj_in_down": proj_in_down, "proj_out_down": proj_out_down, "proj_in_up": proj_in_up, "proj_out_up": proj_out_up, "queries": queries}


def outer_sums(left, right):
    examples = left.shape[0] // SEQ_LEN
    left_f = left.astype(jnp.float32).reshape(examples, SEQ_LEN, left.shape[1])
    right_f = right.astype(jnp.float32).reshape(examples, SEQ_LEN, right.shape[1])
    summed = jnp.einsum("elk,elj->ekj", left_f, right_f, precision=lax.Precision.HIGHEST)
    return summed.reshape(examples, left.shape[1] * right.shape[1])


def reference(gate_preact, up_preact, out_grad, layer_input, w_down, proj_in_down, proj_out_down, proj_in_up, proj_out_up, queries):
    swished = jax.nn.silu(gate_preact.astype(jnp.float32))
    hidden = (swished * up_preact.astype(jnp.float32)).astype(jnp.bfloat16)
    in_down = jnp.dot(hidden, proj_in_down.T, preferred_element_type=jnp.float32)
    out_down = jnp.dot(out_grad, proj_out_down.T, preferred_element_type=jnp.float32).astype(jnp.bfloat16)
    grad_hidden = jnp.dot(out_grad, w_down.T, preferred_element_type=jnp.float32)
    grad_up = (grad_hidden * swished).astype(jnp.bfloat16)
    out_up = jnp.dot(grad_up, proj_out_up.T, preferred_element_type=jnp.float32)
    in_up = jnp.dot(layer_input, proj_in_up.T, preferred_element_type=jnp.float32)
    sketches = jnp.concatenate([outer_sums(out_down, in_down), outer_sums(out_up, in_up)], axis=1).astype(jnp.bfloat16)
    return jnp.dot(sketches, queries.T, preferred_element_type=jnp.float32)
```

```python
import functools

import jax
import jax.numpy as jnp
from jax import lax
from jax.experimental import pallas as pl
from jax.experimental.pallas import tpu as pltpu
from jax.sharding import PartitionSpec as P

SEQ_LEN = 128
F32 = jnp.float32
BF16 = jnp.bfloat16
MESH = pl.DeviceIdType.MESH
HIGHEST = lax.Precision.HIGHEST

CHUNKS = 16
AHEAD = 4
NZ = 4
NDEV = 16
NB = 256


def y_first(chunk):
    return chunk % 5 == 2


def nt(a, b, precision=None):
    return lax.dot_general(
        a, b, (((1,), (1,)), ((), ())), precision=precision, preferred_element_type=F32
    )


def kernel(
    gate_h, up_h, og_h, li_h, w_h, pid_h, pod_h, piu_h, pou_h, q_h,
    out_ref,
    og, w, pod, gate, up, sw, acc, li, piu, pid, pou, qv, odt, ind, iup, rs1, ag1, skp, rs2, tmp, g16, g32,
    own_sem, w_sem, gu_sem, misc_sem, q_sem,
    core_s, core_r, y_s, y_r, up_s, dn_s, zb_r, za_r,
    a2a_s, a2a_r,
):
    rows, width = og_h.shape[0], og.shape[2]
    nblocks = gate.shape[0]
    me = lax.axis_index("dp")
    z, y, core = me // 4, (me // 2) % 2, me % 2
    above, below = me + 4, me - 4
    ypeer = me + 2 - 4 * y
    sibling = me + 1 - 2 * core

    def row(zz, yy):
        return pl.ds(pl.multiple_of((zz * 4 + yy * 2 + core) * rows, rows), rows)

    def push(chunk, where, to, send, recv):
        pltpu.make_async_remote_copy(
            src_ref=og.at[chunk, where], dst_ref=og.at[chunk, where],
            send_sem=send, recv_sem=recv, device_id={"dp": to}, device_id_type=MESH,
        ).start()

    def settle(ref, sem):
        pltpu.make_async_copy(ref, ref, sem).wait()

    def to_core(chunk, where):
        push(chunk, where, sibling, core_s.at[chunk], core_r.at[chunk])

    def to_y(chunk, where):
        push(chunk, where, ypeer, y_s.at[chunk], y_r.at[chunk])

    def to_above(chunk, where, dist):
        @pl.when(z < NZ - 1)
        def _():
            push(chunk, where, above, up_s.at[chunk], zb_r.at[chunk, dist])

    def to_below(chunk, where, dist):
        @pl.when(z > 0)
        def _():
            push(chunk, where, below, dn_s.at[chunk], za_r.at[chunk, dist])

    def everyone(fn):
        def one(k, _):
            fn(lax.rem(me + k, NDEV))
            return 0
        lax.fori_loop(1, NDEV, one, 0)

    def send_all(stage, src_of, dst):
        def one(p):
            pltpu.make_async_remote_copy(
                src_ref=src_of(p), dst_ref=dst.at[me],
                send_sem=a2a_s.at[stage], recv_sem=a2a_r.at[stage],
                device_id={"dp": p}, device_id_type=MESH,
            ).start()
        everyone(one)

    def got_all(stage, dst):
        settle(dst.at[pl.ds(0, NDEV - 1)], a2a_r.at[stage])

    mine = row(z, y)
    for c in range(CHUNKS):
        pltpu.make_async_copy(og_h.at[:, pl.ds(c * width, width)], og.at[c, mine], own_sem).start()
    pltpu.make_async_copy(li_h, li, misc_sem.at[0]).start()
    pltpu.make_async_copy(piu_h, piu, misc_sem.at[1]).start()

    barrier = pltpu.get_barrier_semaphore()
    everyone(lambda p: pl.semaphore_signal(barrier, inc=1, device_id={"dp": p}, device_id_type=MESH))

    settle(og.at[0], own_sem)
    pl.semaphore_wait(barrier, NDEV - 1)

    def send_own(c):
        to_above(c, mine, 0)
        to_below(c, mine, 0)
        to_y(c, mine)
        to_core(c, mine)

    lax.fori_loop(0, AHEAD, lambda c, _: (send_own(c), 0)[1], 0)

    for n in range(nblocks):
        cols = pl.ds(n * NB, NB)
        pltpu.make_async_copy(gate_h.at[:, cols], gate.at[n], gu_sem.at[n]).start()
        pltpu.make_async_copy(up_h.at[:, cols], up.at[n], gu_sem.at[nblocks + n]).start()
        pltpu.make_async_copy(pid_h.at[:, cols], pid.at[n], misc_sem.at[2]).start()
        pltpu.make_async_copy(pou_h.at[:, cols], pou.at[n], misc_sem.at[3]).start()
    for c in range(CHUNKS):
        cols = pl.ds(c * width, width)
        pltpu.make_async_copy(w_h.at[:, cols], w.at[c], w_sem.at[c]).start()
        pltpu.make_async_copy(pod_h.at[:, cols], pod.at[c], w_sem.at[CHUNKS + c]).start()
    pltpu.make_async_copy(q_h, qv, q_sem).start()

    settle(li, misc_sem.at[0])
    settle(piu, misc_sem.at[1])
    twice = jnp.concatenate([piu[...], piu[...]], axis=0)
    part = nt(li[...], twice)
    half = part.shape[0] // 2
    lane = lax.broadcasted_iota(jnp.int32, (half, 128), 1)
    packed = jnp.where(lane < 64, part[:half], part[half:])
    iup[...] = packed.reshape(iup.shape)
    send_all(0, lambda p: iup.at[p], rs1)
    rs1[me] = iup[me]

    acc[...] = jnp.zeros_like(acc)
    odt[...] = jnp.zeros_like(odt)
    ind[...] = jnp.zeros_like(ind)
    settle(pid, misc_sem.at[2])
    settle(pou, misc_sem.at[3])

    def hidden_block(n):
        settle(gate.at[n], gu_sem.at[n])
        settle(up.at[n], gu_sem.at[nblocks + n])
        v = gate[n].astype(F32)
        s = v / (1.0 + jnp.exp(-v))
        sw[n] = s
        hidden = (s * up[n].astype(F32)).astype(BF16)
        pid2 = jnp.concatenate([pid[n], pid[n]], axis=0)
        ind[...] += nt(hidden, pid2)

    def z_stage(c, d):
        first = y_first(c)

        @pl.when(z >= d)
        def _():
            @pl.when(jnp.logical_not(first))
            def _():
                here = row(z - d, y)
                settle(og.at[c, here], zb_r.at[c, d - 1])
                if d < NZ - 1:
                    to_above(c, here, d)
                to_y(c, here)
                to_core(c, here)

            @pl.when(first)
            def _():
                settle(og.at[c, pl.ds(0, 2 * rows)], zb_r.at[c, d - 1])
                for yy in range(2):
                    here = row(z - d, yy)
                    if d < NZ - 1:
                        to_above(c, here, d)
                    to_core(c, here)

        @pl.when(z + d < NZ)
        def _():
            @pl.when(jnp.logical_not(first))
            def _():
                here = row(z + d, y)
                settle(og.at[c, here], za_r.at[c, d - 1])
                if d < NZ - 1:
                    to_below(c, here, d)
                to_y(c, here)
                to_core(c, here)

            @pl.when(first)
            def _():
                settle(og.at[c, pl.ds(0, 2 * rows)], za_r.at[c, d - 1])
                for yy in range(2):
                    here = row(z + d, yy)
                    if d < NZ - 1:
                        to_below(c, here, d)
                    to_core(c, here)

    def y_early(c):
        @pl.when(y_first(c))
        def _():
            here = row(z, 1 - y)
            settle(og.at[c, here], y_r.at[c])
            to_above(c, here, 0)
            to_below(c, here, 0)
            to_core(c, here)

    def y_late(c):
        @pl.when(jnp.logical_not(y_first(c)))
        def _():
            settle(og.at[c, pl.ds(0, NZ * rows)], y_r.at[c])
            for zz in range(NZ):
                to_core(c, row(zz, 1 - y))

    def arrived(c):
        settle(og.at[c, pl.ds(0, 8 * rows)], core_r.at[c])
        settle(w.at[c], w_sem.at[c])
        settle(pod.at[c], w_sem.at[CHUNKS + c])

    def multiply(c):
        arrived(c)

        def one(n, _):
            units = pl.ds(pl.multiple_of(n * NB, NB), NB)
            acc[n] += nt(og[c], w[c, units, :])
            return 0

        lax.fori_loop(0, nblocks, one, 0)
        odt[...] += nt(pod[c], og[c])

    def within(c, fn):
        @pl.when(jnp.logical_and(c >= 0, c < CHUNKS))
        def _():
            fn(c)

    def step(t, _):
        within(t + AHEAD, send_own)
        within(t, y_early)
        within(t, lambda c: z_stage(c, 1))
        within(t - 1, lambda c: z_stage(c, 2))
        within(t - 2, lambda c: z_stage(c, 3))
        within(t - 3, y_late)

        @pl.when(t < nblocks)
        def _():
            hidden_block(t)

        @pl.when(t == 2)
        def _():
            got_all(0, rs1)
            ag1[me] = jnp.sum(rs1[...], axis=0)
            send_all(1, lambda p: ag1.at[me], ag1)

        @pl.when(t >= 4)
        def _():
            multiply(t - 4)

        return 0

    lax.fori_loop(0, CHUNKS + 3, step, 0)

    last = CHUNKS - 1
    got_all(1, ag1)
    arrived(last)

    def finish(n, out_up):
        units = pl.ds(pl.multiple_of(n * NB, NB), NB)
        grad = acc[n] + nt(og[last], w[last, units, :])
        return out_up + nt(pou[n], (grad * sw[n]).astype(BF16))

    out_up = lax.fori_loop(0, nblocks, finish, jnp.zeros(odt.shape, F32))
    out_down = (odt[...] + nt(pod[last], og[last])).astype(BF16).astype(F32)

    examples = out_up.shape[1] // SEQ_LEN
    in_up = ag1[...].reshape(half, 128)
    lane = lax.broadcasted_iota(jnp.int32, (64, 128), 1)
    for e in range(examples):
        toks = slice(e * SEQ_LEN, (e + 1) * SEQ_LEN)
        at = (e * SEQ_LEN) % half
        down = jnp.dot(out_down[:, toks], ind[toks, :], precision=HIGHEST, preferred_element_type=F32)
        ups = jnp.dot(out_up[:, toks], in_up[at:at + SEQ_LEN], precision=HIGHEST, preferred_element_type=F32)
        if e * SEQ_LEN < half:
            ups = pltpu.roll(ups, 64, 1)
        both = jnp.where(lane < 64, down, ups)
        skp[pl.ds(e * 4, 4)] = both.reshape(4, 16, 128)

    send_all(2, lambda p: skp.at[p], rs2)
    rs2[me] = skp[me]
    got_all(2, rs2)
    tmp[...] = jnp.sum(rs2[...], axis=0)
    even = tmp[pl.ds(0, 8, stride=2), :]
    odd = tmp[pl.ds(1, 8, stride=2), :]
    lane = lax.broadcasted_iota(jnp.int32, (8, 128), 1)
    down = jnp.where(lane < 64, even, pltpu.roll(odd, 64, 1))
    ups = jnp.where(lane < 64, pltpu.roll(even, 64, 1), odd)
    g16[me] = jnp.concatenate([down, ups], axis=0).astype(BF16)
    send_all(3, lambda p: g16.at[me], g16)
    settle(qv, q_sem)
    got_all(3, g16)
    g32[...] = g16[...].astype(F32).reshape(g32.shape)
    parts = []
    for half_at in (0, 8):
        for quarter in range(4):
            for r in range(8):
                parts.append(g32[:, quarter, half_at + r, :])
    sketches = jnp.concatenate(parts, axis=1).astype(BF16)
    out_ref[...] = nt(sketches, qv[...])

    def drained(c, _):
        settle(og.at[c, pl.ds(0, 8 * rows)], core_s.at[c])
        first = y_first(c)

        @pl.when(first)
        def _():
            settle(og.at[c, pl.ds(0, rows)], y_s.at[c])

        @pl.when(jnp.logical_not(first))
        def _():
            settle(og.at[c, pl.ds(0, NZ * rows)], y_s.at[c])

        for k in range(NZ - 1):
            for wide in (False, True):
                size = pl.ds(0, (k + 1) * rows * (2 if wide else 1))
                same = first if wide else jnp.logical_not(first)

                @pl.when(jnp.logical_and(same, z == k))
                def _():
                    settle(og.at[c, size], up_s.at[c])

                @pl.when(jnp.logical_and(same, z == NZ - 1 - k))
                def _():
                    settle(og.at[c, size], dn_s.at[c])
        return 0

    lax.fori_loop(0, CHUNKS, drained, 0)
    for stage, dst in enumerate((rs1, ag1, rs2, g16)):
        settle(dst.at[pl.ds(0, NDEV - 1)], a2a_s.at[stage])


def fused(gate, up, out_grad, layer_input, w_down, pid, pod, piu, pou, queries):
    tokens, units = gate.shape
    rows, features = out_grad.shape
    width = features // CHUNKS
    nblocks = units // NB
    examples = tokens // SEQ_LEN
    dma = pltpu.SemaphoreType.DMA
    scratch = [
        pltpu.VMEM((CHUNKS, tokens, width), BF16),
        pltpu.VMEM((CHUNKS, units, width), BF16),
        pltpu.VMEM((CHUNKS, 64, width), BF16),
        pltpu.VMEM((nblocks, tokens, NB), BF16),
        pltpu.VMEM((nblocks, tokens, NB), BF16),
        pltpu.VMEM((nblocks, tokens, NB), F32),
        pltpu.VMEM((nblocks, tokens, NB), F32),
        pltpu.VMEM(layer_input.shape, BF16),
        pltpu.VMEM(piu.shape, BF16),
        pltpu.VMEM((nblocks, 64, NB), BF16),
        pltpu.VMEM((nblocks, 64, NB), BF16),
        pltpu.VMEM(queries.shape, BF16),
        pltpu.VMEM((64, tokens), F32),
        pltpu.VMEM((tokens, 128), F32),
        pltpu.VMEM((NDEV, 16, 128), F32),
        pltpu.VMEM((NDEV, 16, 128), F32),
        pltpu.VMEM((NDEV, 16, 128), F32),
        pltpu.VMEM((NDEV, 16, 128), F32),
        pltpu.VMEM((NDEV, 16, 128), F32),
        pltpu.VMEM((16, 128), F32),
        pltpu.VMEM((NDEV, 16, 128), BF16),
        pltpu.VMEM((examples, 4, 16, 128), F32),
        dma, dma((2 * CHUNKS,)), dma((2 * nblocks,)), dma((4,)), dma,
        dma((CHUNKS,)), dma((CHUNKS,)), dma((CHUNKS,)), dma((CHUNKS,)),
        dma((CHUNKS,)), dma((CHUNKS,)), dma((CHUNKS, NZ - 1)), dma((CHUNKS, NZ - 1)),
        dma((4,)), dma((4,)),
    ]
    return pl.pallas_call(
        kernel,
        out_shape=jax.ShapeDtypeStruct((examples, queries.shape[0]), F32),
        in_specs=[pl.BlockSpec(memory_space=pl.ANY)] * 10,
        out_specs=pl.BlockSpec(memory_space=pltpu.VMEM),
        scratch_shapes=scratch,
        compiler_params=pltpu.CompilerParams(
            collective_id=0, has_side_effects=True, vmem_limit_bytes=60 * 1024 * 1024
        ),
        cost_estimate=pl.CostEstimate(
            flops=2 * tokens * units * features, bytes_accessed=2 * units * features, transcendentals=tokens * units
        ),
    )(gate, up, out_grad, layer_input, w_down, pid, pod, piu, pou, queries)


def outer_sums(left, right):
    examples = left.shape[0] // SEQ_LEN
    left_f = left.reshape(examples, SEQ_LEN, left.shape[1])
    right_f = right.reshape(examples, SEQ_LEN, right.shape[1])
    summed = jnp.einsum("elk,elj->ekj", left_f, right_f, precision=HIGHEST)
    return summed.reshape(examples, left.shape[1] * right.shape[1])


def general(gate, up, out_grad, layer_input, w_down, pid, pod, piu, pou, queries):
    swished = jax.nn.silu(gate.astype(F32))
    hidden = (swished * up.astype(F32)).astype(BF16)
    in_down = nt(hidden, pid)
    in_up = lax.psum(nt(layer_input, piu), "dp")
    piece = lax.all_gather(out_grad, "dp", axis=0, tiled=True)
    out_down = lax.optimization_barrier(nt(piece, pod).astype(BF16)).astype(F32)
    grad_up = (nt(piece, w_down) * swished).astype(BF16)
    out_up = nt(grad_up, pou)
    partial_sketch = jnp.concatenate([outer_sums(out_down, in_down), outer_sums(out_up, in_up)], axis=1)
    sketches = lax.psum(partial_sketch, "dp").astype(BF16)
    return nt(sketches, queries)


def solution(mesh):
    in_specs = (
        P("groups", "dp"),
        P("groups", "dp"),
        P(("groups", "dp"), None),
        P("groups", "dp"),
        P("dp", None),
        P(None, "dp"),
        P(),
        P(None, "dp"),
        P(None, "dp"),
        P("dp", None),
    )
    out_specs = P("groups", "dp")
    body = fused if mesh.shape["dp"] == NDEV else general
    return jax.shard_map(body, mesh=mesh, in_specs=in_specs, out_specs=out_specs, check_vma=False)
```

```python
import functools

import jax
import jax.numpy as jnp
from jax import lax
from jax.experimental import pallas as pl
from jax.experimental.pallas import tpu as pltpu
from jax.sharding import PartitionSpec as P

SEQ_LEN = 128
F32 = jnp.float32
BF16 = jnp.bfloat16
MESH = pl.DeviceIdType.MESH
HIGHEST = lax.Precision.HIGHEST

CHUNKS = 16
AHEAD = 4
NZ = 4
NDEV = 16
NB = 256


def y_first(chunk):
    return chunk % 5 == 2


def nt(a, b, precision=None):
    return lax.dot_general(
        a, b, (((1,), (1,)), ((), ())), precision=precision, preferred_element_type=F32
    )


def kernel(
    gate_h, up_h, og_h, li_h, w_h, pid_h, pod_h, piu_h, pou_h, q_h,
    out_ref,
    og, w, gate, up, sw, acc, li, piu, pid, pou, qv, ind, iup, rs1, ag1, skp, rs2, tmp, g16, g32,
    own_sem, w_sem, gu_sem, misc_sem, q_sem,
    core_s, core_r, y_s, y_r, up_s, dn_s, zb_r, za_r,
    a2a_s, a2a_r,
):
    rows, width = og_h.shape[0], og.shape[2]
    nblocks = gate.shape[0]
    side = pod_h.shape[0]
    me = lax.axis_index("dp")
    z, y, core = me // 4, (me // 2) % 2, me % 2
    above, below = me + 4, me - 4
    ypeer = me + 2 - 4 * y
    sibling = me + 1 - 2 * core

    def row(zz, yy):
        return pl.ds(pl.multiple_of((zz * 4 + yy * 2 + core) * rows, rows), rows)

    def push(chunk, where, to, send, recv):
        pltpu.make_async_remote_copy(
            src_ref=og.at[chunk, where], dst_ref=og.at[chunk, where],
            send_sem=send, recv_sem=recv, device_id={"dp": to}, device_id_type=MESH,
        ).start()

    def settle(ref, sem):
        pltpu.make_async_copy(ref, ref, sem).wait()

    def to_core(chunk, where):
        push(chunk, where, sibling, core_s.at[chunk], core_r.at[chunk])

    def to_y(chunk, where):
        push(chunk, where, ypeer, y_s.at[chunk], y_r.at[chunk])

    def to_above(chunk, where, dist):
        @pl.when(z < NZ - 1)
        def _():
            push(chunk, where, above, up_s.at[chunk], zb_r.at[chunk, dist])

    def to_below(chunk, where, dist):
        @pl.when(z > 0)
        def _():
            push(chunk, where, below, dn_s.at[chunk], za_r.at[chunk, dist])

    def everyone(fn):
        def one(k, _):
            fn(lax.rem(me + k, NDEV))
            return 0
        lax.fori_loop(1, NDEV, one, 0)

    def send_all(stage, src_of, dst):
        def one(p):
            pltpu.make_async_remote_copy(
                src_ref=src_of(p), dst_ref=dst.at[me],
                send_sem=a2a_s.at[stage], recv_sem=a2a_r.at[stage],
                device_id={"dp": p}, device_id_type=MESH,
            ).start()
        everyone(one)

    def got_all(stage, dst):
        settle(dst.at[pl.ds(0, NDEV - 1)], a2a_r.at[stage])

    mine = row(z, y)
    for c in range(CHUNKS):
        pltpu.make_async_copy(og_h.at[:, pl.ds(c * width, width)], og.at[c, mine], own_sem).start()
    pltpu.make_async_copy(li_h, li, misc_sem.at[0]).start()
    pltpu.make_async_copy(piu_h, piu, misc_sem.at[1]).start()

    barrier = pltpu.get_barrier_semaphore()
    everyone(lambda p: pl.semaphore_signal(barrier, inc=1, device_id={"dp": p}, device_id_type=MESH))

    settle(og.at[0, pl.ds(0, CHUNKS * rows)], own_sem)
    pl.semaphore_wait(barrier, NDEV - 1)

    def send_own(c):
        to_above(c, mine, 0)
        to_below(c, mine, 0)
        to_y(c, mine)
        to_core(c, mine)

    lax.fori_loop(0, AHEAD, lambda c, _: (send_own(c), 0)[1], 0)

    for n in range(nblocks):
        cols = pl.ds(n * NB, NB)
        pltpu.make_async_copy(gate_h.at[:, cols], gate.at[n], gu_sem.at[n]).start()
        pltpu.make_async_copy(up_h.at[:, cols], up.at[n], gu_sem.at[nblocks + n]).start()
        pltpu.make_async_copy(pid_h.at[:, cols], pid.at[n], misc_sem.at[2]).start()
        pltpu.make_async_copy(pou_h.at[:, cols], pou.at[n], misc_sem.at[3]).start()
    for c in range(CHUNKS):
        cols = pl.ds(c * width, width)
        pltpu.make_async_copy(pod_h.at[:, cols], w.at[c, pl.ds(0, side)], w_sem.at[c]).start()
        pltpu.make_async_copy(w_h.at[:, cols], w.at[c, pl.ds(side, nblocks * NB)], w_sem.at[c]).start()
    pltpu.make_async_copy(q_h, qv, q_sem).start()

    settle(li, misc_sem.at[0])
    settle(piu, misc_sem.at[1])
    twice = jnp.concatenate([piu[...], piu[...]], axis=0)
    part = nt(li[...], twice)
    half = part.shape[0] // 2
    lane = lax.broadcasted_iota(jnp.int32, (half, 128), 1)
    packed = jnp.where(lane < 64, part[:half], part[half:])
    iup[...] = packed.reshape(iup.shape)
    send_all(0, lambda p: iup.at[p], rs1)
    rs1[me] = iup[me]

    acc[...] = jnp.zeros_like(acc)
    ind[...] = jnp.zeros_like(ind)
    settle(pid, misc_sem.at[2])
    settle(pou, misc_sem.at[3])

    def hidden_block(n):
        settle(gate.at[n], gu_sem.at[n])
        settle(up.at[n], gu_sem.at[nblocks + n])
        v = gate[n].astype(F32)
        s = v / (1.0 + jnp.exp(-v))
        sw[n] = s.T
        hidden = (s * up[n].astype(F32)).astype(BF16)
        pid2 = jnp.concatenate([pid[n], pid[n]], axis=0)
        ind[...] += nt(hidden, pid2)

    def z_stage(c, d):
        first = y_first(c)

        @pl.when(z >= d)
        def _():
            @pl.when(jnp.logical_not(first))
            def _():
                here = row(z - d, y)
                settle(og.at[c, here], zb_r.at[c, d - 1])
                if d < NZ - 1:
                    to_above(c, here, d)
                to_y(c, here)
                to_core(c, here)

            @pl.when(first)
            def _():
                settle(og.at[c, pl.ds(0, 2 * rows)], zb_r.at[c, d - 1])
                for yy in range(2):
                    here = row(z - d, yy)
                    if d < NZ - 1:
                        to_above(c, here, d)
                    to_core(c, here)

        @pl.when(z + d < NZ)
        def _():
            @pl.when(jnp.logical_not(first))
            def _():
                here = row(z + d, y)
                settle(og.at[c, here], za_r.at[c, d - 1])
                if d < NZ - 1:
                    to_below(c, here, d)
                to_y(c, here)
                to_core(c, here)

            @pl.when(first)
            def _():
                settle(og.at[c, pl.ds(0, 2 * rows)], za_r.at[c, d - 1])
                for yy in range(2):
                    here = row(z + d, yy)
                    if d < NZ - 1:
                        to_below(c, here, d)
                    to_core(c, here)

    def y_early(c):
        @pl.when(y_first(c))
        def _():
            here = row(z, 1 - y)
            settle(og.at[c, here], y_r.at[c])
            to_above(c, here, 0)
            to_below(c, here, 0)
            to_core(c, here)

    def y_late(c):
        @pl.when(jnp.logical_not(y_first(c)))
        def _():
            settle(og.at[c, pl.ds(0, NZ * rows)], y_r.at[c])
            for zz in range(NZ):
                to_core(c, row(zz, 1 - y))

    def arrived(c):
        settle(og.at[c, pl.ds(0, 8 * rows)], core_r.at[c])
        settle(w.at[c], w_sem.at[c])

    def multiply(c):
        arrived(c)

        acc[...] += nt(w[c], og[c])

    def within(c, fn):
        @pl.when(jnp.logical_and(c >= 0, c < CHUNKS))
        def _():
            fn(c)

    def step(t, _):
        within(t + AHEAD, send_own)
        within(t + 2, y_early)
        within(t, lambda c: z_stage(c, 1))
        within(t - 2, lambda c: z_stage(c, 2))
        within(t - 4, lambda c: z_stage(c, 3))
        within(t - 6, y_late)

        @pl.when(t < nblocks)
        def _():
            hidden_block(t)

        @pl.when(t == 7)
        def _():
            got_all(0, rs1)
            ag1[me] = jnp.sum(rs1[...], axis=0)
            send_all(1, lambda p: ag1.at[me], ag1)

        @pl.when(t >= 8)
        def _():
            multiply(t - 8)

        return 0

    lax.fori_loop(0, CHUNKS + 7, step, 0)

    last = CHUNKS - 1
    got_all(1, ag1)
    arrived(last)

    acc[...] += nt(w[last], og[last])
    out_down = acc[pl.ds(0, side), :].astype(BF16).astype(F32)
    out_up = jnp.zeros(out_down.shape, F32)
    for n in range(nblocks):
        grad = (acc[pl.ds(side + n * NB, NB), :] * sw[n]).astype(BF16)
        out_up += jnp.dot(pou[n], grad, preferred_element_type=F32)

    examples = out_up.shape[1] // SEQ_LEN
    in_up = ag1[...].reshape(half, 128)
    lane = lax.broadcasted_iota(jnp.int32, (64, 128), 1)
    for e in range(examples):
        toks = slice(e * SEQ_LEN, (e + 1) * SEQ_LEN)
        at = (e * SEQ_LEN) % half
        down = jnp.dot(out_down[:, toks], ind[toks, :], precision=HIGHEST, preferred_element_type=F32)
        ups = jnp.dot(out_up[:, toks], in_up[at:at + SEQ_LEN], precision=HIGHEST, preferred_element_type=F32)
        if e * SEQ_LEN < half:
            ups = pltpu.roll(ups, 64, 1)
        both = jnp.where(lane < 64, down, ups)
        skp[pl.ds(e * 4, 4)] = both.reshape(4, 16, 128)

    send_all(2, lambda p: skp.at[p], rs2)
    rs2[me] = skp[me]
    got_all(2, rs2)
    tmp[...] = jnp.sum(rs2[...], axis=0)
    even = tmp[pl.ds(0, 8, stride=2), :]
    odd = tmp[pl.ds(1, 8, stride=2), :]
    lane = lax.broadcasted_iota(jnp.int32, (8, 128), 1)
    down = jnp.where(lane < 64, even, pltpu.roll(odd, 64, 1))
    ups = jnp.where(lane < 64, pltpu.roll(even, 64, 1), odd)
    g16[me] = jnp.concatenate([down, ups], axis=0).astype(BF16)
    send_all(3, lambda p: g16.at[me], g16)
    settle(qv, q_sem)
    got_all(3, g16)
    g32[...] = g16[...].astype(F32).reshape(g32.shape)
    parts = []
    for half_at in (0, 8):
        for quarter in range(4):
            for r in range(8):
                parts.append(g32[:, quarter, half_at + r, :])
    sketches = jnp.concatenate(parts, axis=1).astype(BF16)
    out_ref[...] = nt(sketches, qv[...])

    def drained(c, _):
        settle(og.at[c, pl.ds(0, 8 * rows)], core_s.at[c])
        first = y_first(c)

        @pl.when(first)
        def _():
            settle(og.at[c, pl.ds(0, rows)], y_s.at[c])

        @pl.when(jnp.logical_not(first))
        def _():
            settle(og.at[c, pl.ds(0, NZ * rows)], y_s.at[c])

        for k in range(NZ - 1):
            for wide in (False, True):
                size = pl.ds(0, (k + 1) * rows * (2 if wide else 1))
                same = first if wide else jnp.logical_not(first)

                @pl.when(jnp.logical_and(same, z == k))
                def _():
                    settle(og.at[c, size], up_s.at[c])

                @pl.when(jnp.logical_and(same, z == NZ - 1 - k))
                def _():
                    settle(og.at[c, size], dn_s.at[c])
        return 0

    lax.fori_loop(0, CHUNKS, drained, 0)
    for stage, dst in enumerate((rs1, ag1, rs2, g16)):
        settle(dst.at[pl.ds(0, NDEV - 1)], a2a_s.at[stage])


def fused(gate, up, out_grad, layer_input, w_down, pid, pod, piu, pou, queries):
    tokens, units = gate.shape
    rows, features = out_grad.shape
    width = features // CHUNKS
    nblocks = units // NB
    examples = tokens // SEQ_LEN
    dma = pltpu.SemaphoreType.DMA
    scratch = [
        pltpu.VMEM((CHUNKS, tokens, width), BF16),
        pltpu.VMEM((CHUNKS, 64 + units, width), BF16),
        pltpu.VMEM((nblocks, tokens, NB), BF16),
        pltpu.VMEM((nblocks, tokens, NB), BF16),
        pltpu.VMEM((nblocks, NB, tokens), F32),
        pltpu.VMEM((64 + units, tokens), F32),
        pltpu.VMEM(layer_input.shape, BF16),
        pltpu.VMEM(piu.shape, BF16),
        pltpu.VMEM((nblocks, 64, NB), BF16),
        pltpu.VMEM((nblocks, 64, NB), BF16),
        pltpu.VMEM(queries.shape, BF16),
        pltpu.VMEM((tokens, 128), F32),
        pltpu.VMEM((NDEV, 16, 128), F32),
        pltpu.VMEM((NDEV, 16, 128), F32),
        pltpu.VMEM((NDEV, 16, 128), F32),
        pltpu.VMEM((NDEV, 16, 128), F32),
        pltpu.VMEM((NDEV, 16, 128), F32),
        pltpu.VMEM((16, 128), F32),
        pltpu.VMEM((NDEV, 16, 128), BF16),
        pltpu.VMEM((examples, 4, 16, 128), F32),
        dma, dma((CHUNKS,)), dma((2 * nblocks,)), dma((4,)), dma,
        dma((CHUNKS,)), dma((CHUNKS,)), dma((CHUNKS,)), dma((CHUNKS,)),
        dma((CHUNKS,)), dma((CHUNKS,)), dma((CHUNKS, NZ - 1)), dma((CHUNKS, NZ - 1)),
        dma((4,)), dma((4,)),
    ]
    return pl.pallas_call(
        kernel,
        out_shape=jax.ShapeDtypeStruct((examples, queries.shape[0]), F32),
        in_specs=[pl.BlockSpec(memory_space=pl.ANY)] * 10,
        out_specs=pl.BlockSpec(memory_space=pltpu.VMEM),
        scratch_shapes=scratch,
        compiler_params=pltpu.CompilerParams(
            collective_id=0, has_side_effects=True, vmem_limit_bytes=60 * 1024 * 1024
        ),
        cost_estimate=pl.CostEstimate(
            flops=2 * tokens * units * features, bytes_accessed=2 * units * features, transcendentals=tokens * units
        ),
    )(gate, up, out_grad, layer_input, w_down, pid, pod, piu, pou, queries)


def outer_sums(left, right):
    examples = left.shape[0] // SEQ_LEN
    left_f = left.reshape(examples, SEQ_LEN, left.shape[1])
    right_f = right.reshape(examples, SEQ_LEN, right.shape[1])
    summed = jnp.einsum("elk,elj->ekj", left_f, right_f, precision=HIGHEST)
    return summed.reshape(examples, left.shape[1] * right.shape[1])


def general(gate, up, out_grad, layer_input, w_down, pid, pod, piu, pou, queries):
    swished = jax.nn.silu(gate.astype(F32))
    hidden = (swished * up.astype(F32)).astype(BF16)
    in_down = nt(hidden, pid)
    in_up = lax.psum(nt(layer_input, piu), "dp")
    piece = lax.all_gather(out_grad, "dp", axis=0, tiled=True)
    out_down = lax.optimization_barrier(nt(piece, pod).astype(BF16)).astype(F32)
    grad_up = (nt(piece, w_down) * swished).astype(BF16)
    out_up = nt(grad_up, pou)
    partial_sketch = jnp.concatenate([outer_sums(out_down, in_down), outer_sums(out_up, in_up)], axis=1)
    sketches = lax.psum(partial_sketch, "dp").astype(BF16)
    return nt(sketches, queries)


def solution(mesh):
    in_specs = (
        P("groups", "dp"),
        P("groups", "dp"),
        P(("groups", "dp"), None),
        P("groups", "dp"),
        P("dp", None),
        P(None, "dp"),
        P(),
        P(None, "dp"),
        P(None, "dp"),
        P("dp", None),
    )
    out_specs = P("groups", "dp")
    body = fused if mesh.shape["dp"] == NDEV else general
    return jax.shard_map(body, mesh=mesh, in_specs=in_specs, out_specs=out_specs, check_vma=False)
```

```python
import functools

import jax
import jax.numpy as jnp
from jax import lax
from jax.experimental import pallas as pl
from jax.experimental.pallas import tpu as pltpu
from jax.sharding import PartitionSpec as P

SEQ_LEN = 128
F32 = jnp.float32
BF16 = jnp.bfloat16
MESH = pl.DeviceIdType.MESH
HIGHEST = lax.Precision.HIGHEST

CHUNKS = 8
AHEAD = 6
NZ = 4
NDEV = 16
NB = 256


def y_first(chunk):
    return chunk % 8 == 4


def nt(a, b, precision=None):
    return lax.dot_general(
        a, b, (((1,), (1,)), ((), ())), precision=precision, preferred_element_type=F32
    )


def kernel(
    gate_h, up_h, og_h, li_h, w_h, pid_h, pod_h, piu_h, pou_h, q_h,
    out_ref,
    og, w, gate, up, sw, acc, li, piu, pid, pou, qv, ind, iup, rs1, ag1, skp, rs2, tmp, g16, g32,
    own_sem, w_sem, gu_sem, misc_sem, q_sem,
    core_s, core_r, y_s, y_r, up_s, dn_s, zb_r, za_r,
    a2a_s, a2a_r,
):
    rows, width = og_h.shape[0], og.shape[2]
    nblocks = gate.shape[0]
    side = pod_h.shape[0]
    me = lax.axis_index("dp")
    z, y, core = me // 4, (me // 2) % 2, me % 2
    above, below = me + 4, me - 4
    ypeer = me + 2 - 4 * y
    sibling = me + 1 - 2 * core

    def row(zz, yy):
        return pl.ds(pl.multiple_of((zz * 4 + yy * 2 + core) * rows, rows), rows)

    def push(chunk, where, to, send, recv):
        pltpu.make_async_remote_copy(
            src_ref=og.at[chunk, where], dst_ref=og.at[chunk, where],
            send_sem=send, recv_sem=recv, device_id={"dp": to}, device_id_type=MESH,
        ).start()

    def settle(ref, sem):
        pltpu.make_async_copy(ref, ref, sem).wait()

    def to_core(chunk, where):
        push(chunk, where, sibling, core_s.at[chunk], core_r.at[chunk])

    def to_y(chunk, where):
        push(chunk, where, ypeer, y_s.at[chunk], y_r.at[chunk])

    def to_above(chunk, where, dist):
        @pl.when(z < NZ - 1)
        def _():
            push(chunk, where, above, up_s.at[chunk], zb_r.at[chunk, dist])

    def to_below(chunk, where, dist):
        @pl.when(z > 0)
        def _():
            push(chunk, where, below, dn_s.at[chunk], za_r.at[chunk, dist])

    def everyone(fn):
        def one(k, _):
            fn(lax.rem(me + k, NDEV))
            return 0
        lax.fori_loop(1, NDEV, one, 0)

    def send_all(stage, src_of, dst):
        def one(p):
            pltpu.make_async_remote_copy(
                src_ref=src_of(p), dst_ref=dst.at[me],
                send_sem=a2a_s.at[stage], recv_sem=a2a_r.at[stage],
                device_id={"dp": p}, device_id_type=MESH,
            ).start()
        everyone(one)

    def got_all(stage, dst):
        settle(dst.at[pl.ds(0, NDEV - 1)], a2a_r.at[stage])

    mine = row(z, y)
    for c in range(CHUNKS):
        pltpu.make_async_copy(og_h.at[:, pl.ds(c * width, width)], og.at[c, mine], own_sem).start()
    pltpu.make_async_copy(li_h, li, misc_sem.at[0]).start()
    pltpu.make_async_copy(piu_h, piu, misc_sem.at[1]).start()

    barrier = pltpu.get_barrier_semaphore()
    everyone(lambda p: pl.semaphore_signal(barrier, inc=1, device_id={"dp": p}, device_id_type=MESH))

    settle(og.at[0, pl.ds(0, CHUNKS * rows)], own_sem)
    pl.semaphore_wait(barrier, NDEV - 1)

    def send_own(c):
        to_above(c, mine, 0)
        to_below(c, mine, 0)
        to_y(c, mine)
        to_core(c, mine)

    lax.fori_loop(0, AHEAD, lambda c, _: (send_own(c), 0)[1], 0)

    for n in range(nblocks):
        cols = pl.ds(n * NB, NB)
        pltpu.make_async_copy(gate_h.at[:, cols], gate.at[n], gu_sem.at[n]).start()
        pltpu.make_async_copy(up_h.at[:, cols], up.at[n], gu_sem.at[nblocks + n]).start()
        pltpu.make_async_copy(pid_h.at[:, cols], pid.at[n], misc_sem.at[2]).start()
        pltpu.make_async_copy(pou_h.at[:, cols], pou.at[n], misc_sem.at[3]).start()
    for c in range(CHUNKS):
        cols = pl.ds(c * width, width)
        pltpu.make_async_copy(pod_h.at[:, cols], w.at[c, pl.ds(0, side)], w_sem.at[c]).start()
        pltpu.make_async_copy(w_h.at[:, cols], w.at[c, pl.ds(side, nblocks * NB)], w_sem.at[c]).start()
    pltpu.make_async_copy(q_h, qv, q_sem).start()

    settle(li, misc_sem.at[0])
    settle(piu, misc_sem.at[1])
    twice = jnp.concatenate([piu[...], piu[...]], axis=0)
    part = nt(li[...], twice)
    half = part.shape[0] // 2
    lane = lax.broadcasted_iota(jnp.int32, (half, 128), 1)
    packed = jnp.where(lane < 64, part[:half], part[half:])
    iup[...] = packed.reshape(iup.shape)
    send_all(0, lambda p: iup.at[p], rs1)
    rs1[me] = iup[me]

    acc[...] = jnp.zeros_like(acc)
    ind[...] = jnp.zeros_like(ind)
    settle(pid, misc_sem.at[2])
    settle(pou, misc_sem.at[3])

    def hidden_block(n):
        settle(gate.at[n], gu_sem.at[n])
        settle(up.at[n], gu_sem.at[nblocks + n])
        v = gate[n].astype(F32)
        s = v / (1.0 + jnp.exp(-v))
        sw[n] = s.T
        hidden = (s * up[n].astype(F32)).astype(BF16)
        pid2 = jnp.concatenate([pid[n], pid[n]], axis=0)
        ind[...] += nt(hidden, pid2)

    def z_stage(c, d):
        first = y_first(c)

        @pl.when(z >= d)
        def _():
            @pl.when(jnp.logical_not(first))
            def _():
                here = row(z - d, y)
                settle(og.at[c, here], zb_r.at[c, d - 1])
                if d < NZ - 1:
                    to_above(c, here, d)
                to_y(c, here)
                to_core(c, here)

            @pl.when(first)
            def _():
                settle(og.at[c, pl.ds(0, 2 * rows)], zb_r.at[c, d - 1])
                for yy in range(2):
                    here = row(z - d, yy)
                    if d < NZ - 1:
                        to_above(c, here, d)
                    to_core(c, here)

        @pl.when(z + d < NZ)
        def _():
            @pl.when(jnp.logical_not(first))
            def _():
                here = row(z + d, y)
                settle(og.at[c, here], za_r.at[c, d - 1])
                if d < NZ - 1:
                    to_below(c, here, d)
                to_y(c, here)
                to_core(c, here)

            @pl.when(first)
            def _():
                settle(og.at[c, pl.ds(0, 2 * rows)], za_r.at[c, d - 1])
                for yy in range(2):
                    here = row(z + d, yy)
                    if d < NZ - 1:
                        to_below(c, here, d)
                    to_core(c, here)

    def y_early(c):
        @pl.when(y_first(c))
        def _():
            here = row(z, 1 - y)
            settle(og.at[c, here], y_r.at[c])
            to_above(c, here, 0)
            to_below(c, here, 0)
            to_core(c, here)

    def y_late(c):
        @pl.when(jnp.logical_not(y_first(c)))
        def _():
            settle(og.at[c, pl.ds(0, NZ * rows)], y_r.at[c])
            for zz in range(NZ):
                to_core(c, row(zz, 1 - y))

    def arrived(c):
        settle(og.at[c, pl.ds(0, 8 * rows)], core_r.at[c])
        settle(w.at[c], w_sem.at[c])

    def add_product(c):
        def one(k, _):
            part = pl.ds(pl.multiple_of(k * 512, 512), 512)
            acc[...] += nt(w[c, :, part], og[c, :, part])
            return 0

        lax.fori_loop(0, width // 512, one, 0)

    def multiply(c):
        arrived(c)

        add_product(c)

    def within(c, fn):
        @pl.when(jnp.logical_and(c >= 0, c < CHUNKS))
        def _():
            fn(c)

    def step(t, _):
        within(t + AHEAD, send_own)
        within(t + 2, y_early)
        within(t, lambda c: z_stage(c, 1))
        within(t - 1, lambda c: z_stage(c, 2))
        within(t - 2, lambda c: z_stage(c, 3))
        within(t - 3, y_late)

        @pl.when(t < nblocks)
        def _():
            hidden_block(t)

        @pl.when(t == 7)
        def _():
            got_all(0, rs1)
            ag1[me] = jnp.sum(rs1[...], axis=0)
            send_all(1, lambda p: ag1.at[me], ag1)

        @pl.when(t >= 4)
        def _():
            multiply(t - 4)

        return 0

    lax.fori_loop(0, CHUNKS + 3, step, 0)

    last = CHUNKS - 1
    got_all(1, ag1)
    arrived(last)

    add_product(last)
    out_down = acc[pl.ds(0, side), :].astype(BF16).astype(F32)
    out_up = jnp.zeros(out_down.shape, F32)
    for n in range(nblocks):
        grad = (acc[pl.ds(side + n * NB, NB), :] * sw[n]).astype(BF16)
        out_up += jnp.dot(pou[n], grad, preferred_element_type=F32)

    examples = out_up.shape[1] // SEQ_LEN
    in_up = ag1[...].reshape(half, 128)
    lane = lax.broadcasted_iota(jnp.int32, (64, 128), 1)
    for e in range(examples):
        toks = slice(e * SEQ_LEN, (e + 1) * SEQ_LEN)
        at = (e * SEQ_LEN) % half
        down = jnp.dot(out_down[:, toks], ind[toks, :], precision=HIGHEST, preferred_element_type=F32)
        ups = jnp.dot(out_up[:, toks], in_up[at:at + SEQ_LEN], precision=HIGHEST, preferred_element_type=F32)
        if e * SEQ_LEN < half:
            ups = pltpu.roll(ups, 64, 1)
        both = jnp.where(lane < 64, down, ups)
        skp[pl.ds(e * 4, 4)] = both.reshape(4, 16, 128)

    send_all(2, lambda p: skp.at[p], rs2)
    rs2[me] = skp[me]
    got_all(2, rs2)
    tmp[...] = jnp.sum(rs2[...], axis=0)
    even = tmp[pl.ds(0, 8, stride=2), :]
    odd = tmp[pl.ds(1, 8, stride=2), :]
    lane = lax.broadcasted_iota(jnp.int32, (8, 128), 1)
    down = jnp.where(lane < 64, even, pltpu.roll(odd, 64, 1))
    ups = jnp.where(lane < 64, pltpu.roll(even, 64, 1), odd)
    g16[me] = jnp.concatenate([down, ups], axis=0).astype(BF16)
    send_all(3, lambda p: g16.at[me], g16)
    settle(qv, q_sem)
    got_all(3, g16)
    g32[...] = g16[...].astype(F32).reshape(g32.shape)
    parts = []
    for half_at in (0, 8):
        for quarter in range(4):
            for r in range(8):
                parts.append(g32[:, quarter, half_at + r, :])
    sketches = jnp.concatenate(parts, axis=1).astype(BF16)
    out_ref[...] = nt(sketches, qv[...])

    def drained(c, _):
        settle(og.at[c, pl.ds(0, 8 * rows)], core_s.at[c])
        first = y_first(c)

        @pl.when(first)
        def _():
            settle(og.at[c, pl.ds(0, rows)], y_s.at[c])

        @pl.when(jnp.logical_not(first))
        def _():
            settle(og.at[c, pl.ds(0, NZ * rows)], y_s.at[c])

        for k in range(NZ - 1):
            for wide in (False, True):
                size = pl.ds(0, (k + 1) * rows * (2 if wide else 1))
                same = first if wide else jnp.logical_not(first)

                @pl.when(jnp.logical_and(same, z == k))
                def _():
                    settle(og.at[c, size], up_s.at[c])

                @pl.when(jnp.logical_and(same, z == NZ - 1 - k))
                def _():
                    settle(og.at[c, size], dn_s.at[c])
        return 0

    lax.fori_loop(0, CHUNKS, drained, 0)
    for stage, dst in enumerate((rs1, ag1, rs2, g16)):
        settle(dst.at[pl.ds(0, NDEV - 1)], a2a_s.at[stage])


def fused(gate, up, out_grad, layer_input, w_down, pid, pod, piu, pou, queries):
    tokens, units = gate.shape
    rows, features = out_grad.shape
    width = features // CHUNKS
    nblocks = units // NB
    examples = tokens // SEQ_LEN
    dma = pltpu.SemaphoreType.DMA
    scratch = [
        pltpu.VMEM((CHUNKS, tokens, width), BF16),
        pltpu.VMEM((CHUNKS, 64 + units, width), BF16),
        pltpu.VMEM((nblocks, tokens, NB), BF16),
        pltpu.VMEM((nblocks, tokens, NB), BF16),
        pltpu.VMEM((nblocks, NB, tokens), F32),
        pltpu.VMEM((64 + units, tokens), F32),
        pltpu.VMEM(layer_input.shape, BF16),
        pltpu.VMEM(piu.shape, BF16),
        pltpu.VMEM((nblocks, 64, NB), BF16),
        pltpu.VMEM((nblocks, 64, NB), BF16),
        pltpu.VMEM(queries.shape, BF16),
        pltpu.VMEM((tokens, 128), F32),
        pltpu.VMEM((NDEV, 16, 128), F32),
        pltpu.VMEM((NDEV, 16, 128), F32),
        pltpu.VMEM((NDEV, 16, 128), F32),
        pltpu.VMEM((NDEV, 16, 128), F32),
        pltpu.VMEM((NDEV, 16, 128), F32),
        pltpu.VMEM((16, 128), F32),
        pltpu.VMEM((NDEV, 16, 128), BF16),
        pltpu.VMEM((examples, 4, 16, 128), F32),
        dma, dma((CHUNKS,)), dma((2 * nblocks,)), dma((4,)), dma,
        dma((CHUNKS,)), dma((CHUNKS,)), dma((CHUNKS,)), dma((CHUNKS,)),
        dma((CHUNKS,)), dma((CHUNKS,)), dma((CHUNKS, NZ - 1)), dma((CHUNKS, NZ - 1)),
        dma((4,)), dma((4,)),
    ]
    return pl.pallas_call(
        kernel,
        out_shape=jax.ShapeDtypeStruct((examples, queries.shape[0]), F32),
        in_specs=[pl.BlockSpec(memory_space=pl.ANY)] * 10,
        out_specs=pl.BlockSpec(memory_space=pltpu.VMEM),
        scratch_shapes=scratch,
        compiler_params=pltpu.CompilerParams(
            collective_id=0, has_side_effects=True, vmem_limit_bytes=60 * 1024 * 1024
        ),
        cost_estimate=pl.CostEstimate(
            flops=2 * tokens * units * features, bytes_accessed=2 * units * features, transcendentals=tokens * units
        ),
    )(gate, up, out_grad, layer_input, w_down, pid, pod, piu, pou, queries)


def outer_sums(left, right):
    examples = left.shape[0] // SEQ_LEN
    left_f = left.reshape(examples, SEQ_LEN, left.shape[1])
    right_f = right.reshape(examples, SEQ_LEN, right.shape[1])
    summed = jnp.einsum("elk,elj->ekj", left_f, right_f, precision=HIGHEST)
    return summed.reshape(examples, left.shape[1] * right.shape[1])


def general(gate, up, out_grad, layer_input, w_down, pid, pod, piu, pou, queries):
    swished = jax.nn.silu(gate.astype(F32))
    hidden = (swished * up.astype(F32)).astype(BF16)
    in_down = nt(hidden, pid)
    in_up = lax.psum(nt(layer_input, piu), "dp")
    piece = lax.all_gather(out_grad, "dp", axis=0, tiled=True)
    out_down = lax.optimization_barrier(nt(piece, pod).astype(BF16)).astype(F32)
    grad_up = (nt(piece, w_down) * swished).astype(BF16)
    out_up = nt(grad_up, pou)
    partial_sketch = jnp.concatenate([outer_sums(out_down, in_down), outer_sums(out_up, in_up)], axis=1)
    sketches = lax.psum(partial_sketch, "dp").astype(BF16)
    return nt(sketches, queries)


def solution(mesh):
    in_specs = (
        P("groups", "dp"),
        P("groups", "dp"),
        P(("groups", "dp"), None),
        P("groups", "dp"),
        P("dp", None),
        P(None, "dp"),
        P(),
        P(None, "dp"),
        P(None, "dp"),
        P("dp", None),
    )
    out_specs = P("groups", "dp")
    body = fused if mesh.shape["dp"] == NDEV else general
    return jax.shard_map(body, mesh=mesh, in_specs=in_specs, out_specs=out_specs, check_vma=False)
```
